32 devices in a mesh: surf: 8 (over z, x), normal: 4 (over y, core).
Axes of the slice: x: 2, y: 2, z: 4, core: 2. Of those that a mesh axis runs over, the one named last changes fastest.
Arguments:
- profile: bfloat16 [16, 16, 131072], P('normal', None, 'surf'), may hold values from -6 to 6
- wall_weight: bfloat16 [10, 16, 16], P(None, 'normal'), may hold values from -0.375 to 0.375
- block_dest: int32 [1024], replicated, may hold values from 0 to 7, as said below
- col_face: int32 [32768], P(('surf', 'normal')), may hold values from 0 to 16383
- char_state: float32 [8, 128, 32768], P(None, None, ('surf', 'normal')), may hold values from -6 to 6
- char_inverse: bfloat16 [128, 128], replicated, as said below
- react: float32 [8, 8], replicated, may hold values from -2 to 2
- bound_weight: float32 [8, 10], replicated, may hold values from -2 to 2
Outputs:
- char_next: float32 [8, 128, 32768], P(None, None, ('surf', 'normal'))
The draws below stay inside these ranges and needn't reach their ends.
Inputs may be any that keep to these rules, and one draw needn't show every extreme that they name: `block_dest`: each block of surface patch s (blocks s * 128 to (s + 1) * 128 - 1) names an owner; no owner is named by more than 32 blocks of one patch, every patch names some owner exactly 32 times, and every owner is named by exactly 128 blocks in all. `char_inverse`: inverse of a diagonally dominant conduction matrix; its norm is below one.
All inputs are finite; a program needn't handle non-finite values.
Results may differ from the reference program's by a relative error of at most 0.0047.
Values sent between devices are 32-bit elements; how exact they have to be, the bound alone decides.
A program may use at most 128 MiB of HBM per device.

```python
import jax
import jax.numpy as jnp
from jax import lax

VARS = 16
OUTC = 10
COMP = 8
DEPTH = 128
BLOCK = 128
STEPS = 8
NB_DEV = 128
MCOL_DEV = 1024
ROWS = 16
NBLK = 1024
FACES = 131072
MCOL = 32768
N_SURF = 8
N_NORMAL = 4


def draw_block_dest(key, part):
    key = jax.random.fold_in(key, 11)
    cap = max(2, 2 * NB_DEV // N_SURF)
    groups = NB_DEV // cap
    order = jax.random.permutation(key, N_SURF).astype(jnp.int32)
    sender = jnp.arange(N_SURF, dtype=jnp.int32)[:, None]
    blocks = jnp.arange(NB_DEV, dtype=jnp.int32)[None, :]
    where_to = (sender * groups + blocks // cap) % N_SURF
    return jnp.take(order, where_to.reshape(-1)).astype(jnp.int32)


def draw_char_inverse(key, part):
    key = jax.random.fold_in(key, 3)
    eye = (jnp.arange(DEPTH)[:, None] == jnp.arange(DEPTH)[None, :]).astype(jnp.float32)
    spread = jnp.clip(jax.random.normal(key, (DEPTH, DEPTH), jnp.float32), -3.0, 3.0)
    return (0.6 * eye + 0.2 * spread / jnp.sqrt(DEPTH * 1.0)).astype(jnp.bfloat16)


def touch_ends(array, own_key, least, top_value):
    longest = array.shape.index(max(array.shape))
    spots = []
    for shift in (0, 1):
        where = [jax.random.randint(jax.random.fold_in(own_key, axis), (), 0, length) for axis, length in enumerate(array.shape)]
        where[longest] = (where[longest] + shift) % array.shape[longest]
        spots.append(tuple(where))
    return array.at[spots[0]].set(least).at[spots[1]].set(top_value)


def levels(key, dims, cuts, smallest, top_value):
    gain, own = 1.0, jax.random.fold_in(key, 6)
    for position, parts in cuts:
        draws = jnp.exp(jax.random.uniform(jax.random.fold_in(own, position), (parts,), jnp.float32, smallest / len(cuts), top_value / len(cuts)))
        gain = gain * jnp.repeat(draws, dims[position] // parts).reshape([-1 if axis == position else 1 for axis in range(len(dims))])
    return gain


def noise(key, dims, width, reach, pieces=(), kind=jnp.bfloat16):
    entries = jax.random.normal(key, dims, jnp.float32) * width
    if len(pieces) > 0:
        entries = levels(key, dims, pieces, -0.22, 0.18) * entries
    return jnp.clip(entries, min=-reach, max=reach).astype(kind)


def setup_inputs(seed: int = 0) -> dict:
    arg_keys = jax.random.split(jax.random.key(seed), 9)
    return {
        "profile": noise(arg_keys[0], (ROWS, VARS, FACES), 1.0, 6.0, ((0, 4), (2, 8))),
        "wall_weight": noise(arg_keys[1], (OUTC, ROWS, VARS), (ROWS * VARS) ** -0.5, 0.375, ((1, 4),)),
        "block_dest": draw_block_dest(jax.random.fold_in(arg_keys[8], 71), 0),
        "col_face": touch_ends(jax.random.randint(arg_keys[3], (MCOL,), 0, NB_DEV * BLOCK), jax.random.fold_in(arg_keys[3], 1), 0, (NB_DEV * BLOCK) - 1).astype(jnp.int32),
        "char_state": noise(arg_keys[4], (COMP, DEPTH, MCOL), 1.0, 6.0, ((2, 32),), jnp.float32),
        "char_inverse": draw_char_inverse(jax.random.fold_in(arg_keys[8], 71), 0),
        "react": noise(arg_keys[6], (COMP, COMP), COMP ** -0.5, 2.0, (), jnp.float32),
        "bound_weight": noise(arg_keys[7], (COMP, OUTC), OUTC ** -0.5, 2.0, (), jnp.float32),
    }


def bounded(raw):
    return raw * lax.rsqrt(1.0 + raw * raw)

def char_steps(state, source, char_inverse, react):
    inverse_wide = char_inverse.astype(jnp.float32)
    lead = inverse_wide[:, 0]
    for step in range(STEPS):
        driven = state + 0.5 * jnp.einsum('ck,kdm->cdm', react, jnp.tanh(state), precision=lax.Precision.HIGHEST)
        driven = driven.astype(jnp.bfloat16).astype(jnp.float32)
        state = jnp.einsum('de,cem->cdm', inverse_wide, driven, precision=lax.Precision.HIGHEST) + lead[None, :, None] * source[:, None, :]
    return state

def reference(profile, wall_weight, block_dest, col_face, char_state, char_inverse, react, bound_weight):
    weights = jnp.transpose(wall_weight.astype(jnp.float32), (1, 0, 2))

    def add_row(total, pair):
        return (total + jnp.dot(pair[0], pair[1].astype(jnp.float32), precision=lax.Precision.HIGHEST), None)
    raw, unused = lax.scan(add_row, jnp.zeros((OUTC, FACES), jnp.float32), (weights, profile))
    wall = bounded(raw)
    onehot = (block_dest[:, None] == jnp.arange(N_SURF, dtype=jnp.int32)[None, :]).astype(jnp.int32)
    before = jnp.cumsum(onehot, axis=0).astype(jnp.int32) - onehot
    rank = lax.optimization_barrier(jnp.sum(before * onehot, axis=1)).astype(jnp.int32)
    where_put = (block_dest * NB_DEV + rank).astype(jnp.int32)
    listing = jnp.zeros((N_SURF * NB_DEV,), jnp.int32).at[where_put].set(jnp.arange(NBLK, dtype=jnp.int32))
    column = jnp.arange(MCOL, dtype=jnp.int32)
    owner = (column // (MCOL_DEV * N_NORMAL)).astype(jnp.int32)
    chosen = jnp.take(listing, (owner * NB_DEV + col_face // BLOCK).astype(jnp.int32))
    face = (chosen * BLOCK + col_face % BLOCK).astype(jnp.int32)
    boundary = jnp.take(wall, face, axis=1)
    source = jnp.dot(bound_weight, boundary, precision=lax.Precision.HIGHEST)
    count = MCOL // MCOL_DEV
    states = jnp.transpose(char_state.reshape(COMP, DEPTH, count, MCOL_DEV), (2, 0, 1, 3))
    sources = jnp.transpose(source.reshape(COMP, count, MCOL_DEV), (1, 0, 2))
    result = lax.map(lambda pair: char_steps(pair[0], pair[1], char_inverse, react), (states, sources))
    return jnp.transpose(result, (1, 2, 0, 3)).reshape(COMP, DEPTH, MCOL)
```

```python
import jax
import jax.numpy as jnp
from jax import lax
from jax.sharding import PartitionSpec as P

import functools
from jax.experimental import pallas as pl
from jax.experimental.pallas import tpu as pltpu

STEPS = 8
F32 = jnp.float32
BF = jnp.bfloat16

def char_kernel(lo, sub, order, mix_ref, inv_ref, lead_ref, src_ref, st_ref, out_ref, t_ref, dr_ref):
    comp, depth, width = st_ref.shape
    grp = 256 // comp
    lead = lead_ref[...]
    for c in range(comp):
        t_ref[c] = jnp.tanh(st_ref[c]).astype(BF)
        out_ref[c] = st_ref[c]
    def step(i, carry):
        def mixp(h):
            ls = slice(h*sub, (h+1)*sub)
            for g in range(depth // grp):
                ds = slice(g*grp, (g+1)*grp)
                t = t_ref[:, ds, ls].reshape(comp*grp, sub)
                if lo:
                    t = jnp.concatenate([t, t], axis=0)
                m = jnp.dot(mix_ref[...], t, preferred_element_type=F32)
                dr_ref[:, ds, ls] = (out_ref[:, ds, ls] + m.reshape(comp, grp, sub)).astype(BF)
        def invp(h):
            ls = slice(h*sub, (h+1)*sub)
            for p in range(comp // 2):
                x = dr_ref[2*p:2*p+2, :, ls].reshape(2*depth, sub)
                y = jnp.dot(inv_ref[...], x, preferred_element_type=F32)
                for k in range(2):
                    c = 2*p+k
                    n = y[k*depth:(k+1)*depth] + lead * src_ref[c:c+1, ls]
                    out_ref[c, :, ls] = n
                    t_ref[c, :, ls] = jnp.tanh(n).astype(BF)
        H = width // sub
        if order == 0:
            for h in range(H): mixp(h)
            for h in range(H): invp(h)
        elif order == 1:
            for h in range(H):
                mixp(h); invp(h)
        return carry
    lax.fori_loop(0, STEPS, step, 0)

def char_steps(char_state, source, char_inverse, react, lo=True, tile=512, sub=256, order=0):
    comp, depth, cols = char_state.shape
    grp = 256 // comp
    half = 0.5*react
    hi = half.astype(BF)
    parts = [hi]
    if lo:
        hi32 = lax.reduce_precision(half, 8, 7)
        parts = [hi32.astype(BF), (half - hi32).astype(BF)]
    eye = jnp.eye(grp, dtype=BF)
    mix = jnp.concatenate([jnp.kron(p, eye) for p in parts], axis=1)
    inv = jnp.kron(jnp.eye(2, dtype=BF), char_inverse)
    lead = char_inverse[:, :1].astype(F32)
    full = lambda a: pl.BlockSpec(a.shape, lambda i: (0,)*a.ndim)
    return pl.pallas_call(
        functools.partial(char_kernel, lo, sub, order),
        grid=(cols//tile,),
        in_specs=[full(mix), full(inv), full(lead), pl.BlockSpec((comp, tile), lambda i:(0,i)), pl.BlockSpec((comp,depth,tile), lambda i:(0,0,i))],
        out_specs=pl.BlockSpec((comp,depth,tile), lambda i:(0,0,i)),
        out_shape=jax.ShapeDtypeStruct(char_state.shape, F32),
        scratch_shapes=[pltpu.VMEM((comp,depth,tile),BF), pltpu.VMEM((comp,depth,tile),BF)],
        compiler_params=pltpu.CompilerParams(vmem_limit_bytes=56*2**20),
        name="char_steps",
    )(mix, inv, lead, source, char_state)

def bounded(raw):
    return raw * lax.rsqrt(1.0 + raw * raw)


def body(profile, wall_weight, block_dest, col_face, char_state, char_inverse, react, bound_weight):
    nsurf = lax.axis_size("surf")
    here = lax.axis_index("surf")
    nblk = profile.shape[2] // 128
    cap = max(2, 2 * nblk // nsurf)
    outc = wall_weight.shape[0]
    partial_value = jnp.einsum(
        "orv,rvf->of", wall_weight, profile, preferred_element_type=jnp.float32
    )
    table = block_dest.reshape(nsurf, nblk)
    earlier = jnp.arange(nblk)[:, None] > jnp.arange(nblk)[None, :]
    same = table[:, :, None] == table[:, None, :]
    slots = jnp.sum(jnp.logical_and(same, earlier[None]).astype(jnp.int32), axis=2)
    mine_dest = lax.dynamic_index_in_dim(table, here, 0, keepdims=False)
    mine_slot = lax.dynamic_index_in_dim(slots, here, 0, keepdims=False)
    target = mine_dest * cap + mine_slot
    placing = (jnp.arange(nsurf * cap)[:, None] == target[None, :]).astype(jnp.float32)
    wall = bounded(lax.psum(partial_value, "normal"))
    payload = wall.reshape(outc, nblk, 128)
    send = jnp.einsum("sb,obw->sow", placing, payload, precision=lax.Precision.HIGHEST)
    arrived = lax.all_to_all(
        send.reshape(nsurf, cap, payload.shape[0], 128),
        "surf",
        split_axis=0,
        concat_axis=0,
        tiled=True,
    )
    counts = jnp.sum((table == here).astype(jnp.int32), axis=1)
    running = jnp.cumsum(counts)
    place = col_face // 128
    within = col_face % 128
    sender = jnp.sum((running[None, :] <= place[:, None]).astype(jnp.int32), axis=1)
    start = jnp.take(running - counts, sender)
    entry = sender * cap + (place - start)
    received = arrived.reshape(nsurf * cap, arrived.shape[2], 128)
    picked = received[entry, :, within]
    source = jnp.einsum("co,mo->cm", bound_weight, picked, precision=lax.Precision.HIGHEST)
    return char_steps(char_state, source, char_inverse, react)


def solution(mesh):
    placed = (
        P("normal", None, "surf"),
        P(None, "normal", None),
        P(),
        P(("surf", "normal")),
        P(None, None, ("surf", "normal")),
        P(),
        P(),
        P(),
    )
    return jax.shard_map(
        body,
        mesh=mesh,
        in_specs=placed,
        out_specs=P(None, None, ("surf", "normal")),
        check_vma=False,
    )
```

```python
import functools

import jax
import jax.numpy as jnp
from jax import lax
from jax.experimental import pallas as pl
from jax.experimental.pallas import tpu as pltpu
from jax.sharding import PartitionSpec as P

STEPS = 8
PIECES = 4
LANES = 128
F32 = jnp.float32
BF = jnp.bfloat16
MESH = pl.DeviceIdType.MESH


def source_kernel(
    nsurf, chips, outc,
    x_ref, w_ref, dest_ref, cf_ref, bw_ref,
    src_ref,
    send_a, own_a, recv_a, chip_b, recv_b, wall_ref, s_ref, cat_ref, key_ref, cf_all, gbuf, rbuf,
    sa_send, sa_recv, sb_send, sb_recv, ss_send, ss_recv, sc_send, sc_recv, sg_send, sg_recv,
):
    surf = lax.axis_index("surf")
    normal = lax.axis_index("normal")
    y, core = normal // 2, normal % 2
    peer = (surf, y * 2 + 1 - core)
    extra = outc - 8
    subs = 8 // extra
    faces = x_ref.shape[2]
    half = faces // 2
    piece = half // PIECES
    sub = piece // subs
    depth = x_ref.shape[0] * x_ref.shape[1]
    nblk = faces // LANES
    groups = piece // LANES

    def chip_peer(k):
        return (surf, lax.rem(y + k, chips) * 2 + core)

    def surf_peer(k):
        return (lax.rem(surf + k, nsurf), normal)

    barrier = pltpu.get_barrier_semaphore()
    pl.semaphore_signal(barrier, inc=1, device_id=peer, device_id_type=MESH)
    for k in range(1, chips):
        pl.semaphore_signal(barrier, inc=1, device_id=chip_peer(k), device_id_type=MESH)

    def greet(k, carry):
        pl.semaphore_signal(barrier, inc=1, device_id=surf_peer(k), device_id_type=MESH)
        return carry

    lax.fori_loop(1, nsurf, greet, 0)

    wide = w_ref[...].astype(F32)
    row = lax.broadcasted_iota(jnp.int32, wide.shape, 0)

    def weights(q):
        keep = jnp.logical_or(row < 8, (row - 8) // extra == q)
        return jnp.where(keep, wide, 0.0).astype(BF)

    placed = [weights(q) for q in range(subs)]

    def partial(which, p):
        rest = None
        main = []
        for q in range(subs):
            start = pl.multiple_of(which * half + p * piece + q * sub, sub)
            x = x_ref[:, :, pl.ds(start, sub)].reshape(depth, sub)
            r = jnp.dot(placed[q], x, preferred_element_type=F32)
            main.append(r[:8])
            rest = r[8:] if rest is None else rest + r[8:]
        return jnp.concatenate(main + [rest], axis=1)

    def copy_a(p):
        return pltpu.make_async_remote_copy(
            src_ref=send_a.at[p], dst_ref=recv_a.at[p], send_sem=sa_send.at[p], recv_sem=sa_recv.at[p],
            device_id=peer, device_id_type=MESH)

    def copy_b(k, p):
        return pltpu.make_async_remote_copy(
            src_ref=chip_b.at[p], dst_ref=recv_b.at[k - 1, p], send_sem=sb_send.at[k - 1, p],
            recv_sem=sb_recv.at[k - 1, p], device_id=chip_peer(k), device_id_type=MESH)

    def copy_s(p):
        start = pl.multiple_of((core * PIECES + p) * groups * 8, groups * 8)
        rows = s_ref.at[pl.ds(start, groups * 8)]
        return pltpu.make_async_remote_copy(
            src_ref=rows, dst_ref=rows, send_sem=ss_send.at[p], recv_sem=ss_recv.at[p],
            device_id=peer, device_id_type=MESH)

    def wait_s(p):
        start = pl.multiple_of(((1 - core) * PIECES + p) * groups * 8, groups * 8)
        rows = s_ref.at[pl.ds(start, groups * 8)]
        return pltpu.make_async_remote_copy(
            src_ref=rows, dst_ref=rows, send_sem=ss_send.at[p], recv_sem=ss_recv.at[p],
            device_id=peer, device_id_type=MESH)

    def copy_c(k):
        return pltpu.make_async_remote_copy(
            src_ref=cf_ref, dst_ref=cf_all.at[k], send_sem=sc_send.at[k], recv_sem=sc_recv.at[k],
            device_id=surf_peer(k), device_id_type=MESH)

    def copy_g(k):
        return pltpu.make_async_remote_copy(
            src_ref=gbuf.at[k], dst_ref=rbuf.at[k], send_sem=sg_send.at[k], recv_sem=sg_recv.at[k],
            device_id=surf_peer(k), device_id_type=MESH)

    send_a[0] = partial(1 - core, 0)
    pl.semaphore_wait(barrier, 1 + chips - 1 + nsurf - 1)
    copy_a(0).start()
    own_a[0] = partial(core, 0)
    for p in range(1, PIECES):
        send_a[p] = partial(1 - core, p)
        copy_a(p).start()
        own_a[p] = partial(core, p)
    for p in range(PIECES):
        copy_a(p).wait_recv()
        chip_b[p] = own_a[p] + recv_a[p]
        for k in range(1, chips):
            copy_b(k, p).start()

    def start_c(k, carry):
        copy_c(k).start()
        return carry

    lax.fori_loop(1, nsurf, start_c, 0)
    cf_all[0] = cf_ref[...]

    line = lax.broadcasted_iota(jnp.int32, (nblk, nblk), 0)
    lane = lax.broadcasted_iota(jnp.int32, (nblk, nblk), 1)
    mine = jnp.broadcast_to(dest_ref[pl.ds(surf, 1), :], (nblk, nblk))
    owner = jnp.sum(jnp.where(line == lane, mine, 0), axis=1, keepdims=True)

    def count(s, total):
        other = jnp.broadcast_to(dest_ref[pl.ds(s, 1), :], (nblk, nblk))
        before = s * nblk + lane < surf * nblk + line
        return total + jnp.where(jnp.logical_and(other == owner, before), 1, 0)

    ranks = lax.fori_loop(0, nsurf, count, jnp.zeros((nblk, nblk), jnp.int32))
    rank = jnp.sum(ranks, axis=1, keepdims=True)
    key_ref[...] = jnp.broadcast_to(owner * nblk + rank, (nblk, LANES))

    bw = bw_ref[...]
    columns = [jnp.broadcast_to(bw[:, o:o + 1], (8, sub)) for o in range(outc)]
    for p in range(PIECES):
        total = chip_b[p]
        for k in range(1, chips):
            copy_b(k, p).wait_recv()
            total = total + recv_b[k - 1, p]
        wall_ref[p] = total * lax.rsqrt(1.0 + total * total)
        for q in range(subs):
            acc = jnp.zeros((8, sub), F32)
            for o in range(outc):
                if o < 8:
                    w = wall_ref[p, o:o + 1, q * sub:(q + 1) * sub]
                else:
                    r = q * extra + o - 8
                    w = wall_ref[p, r:r + 1, piece:piece + sub]
                acc = acc + columns[o] * jnp.broadcast_to(w, (8, sub))
            for i in range(sub // LANES):
                at = (core * PIECES + p) * groups + q * (sub // LANES) + i
                s_ref[pl.ds(pl.multiple_of(at * 8, 8), 8), :] = acc[:, i * LANES:(i + 1) * LANES]
        copy_s(p).start()

    def split(start, rows):
        s = s_ref[pl.ds(start, rows), :]
        hi = s.astype(BF)
        cat_ref[pl.ds(start, rows), :] = jnp.concatenate(
            [hi, (s - hi.astype(F32)).astype(BF)], axis=1)

    for p in range(PIECES):
        split(pl.multiple_of((core * PIECES + p) * groups * 8, groups * 8), groups * 8)

    def wait_c(k, carry):
        copy_c(k).wait()
        return carry

    lax.fori_loop(1, nsurf, wait_c, 0)
    for p in range(PIECES):
        wait_s(p).wait_recv()
        split(pl.multiple_of(((1 - core) * PIECES + p) * groups * 8, groups * 8), groups * 8)

    tiles = cf_ref.shape[0]
    cols = tiles * LANES
    within = lax.broadcasted_iota(jnp.int32, (LANES, LANES), 0)
    chunk = 32

    def pick(k):
        who = lax.rem(surf + k, nsurf)
        cf = cf_all[lax.rem(nsurf - k, nsurf)]
        place = who * nblk + cf // LANES
        spot = cf % LANES
        onehot = jnp.concatenate(
            [jnp.where(within == spot[j:j + 1, :], 1.0, 0.0).astype(BF) for j in range(tiles)], axis=1)
        onehot = jnp.concatenate([onehot, onehot], axis=0)
        want = jnp.concatenate(
            [jnp.broadcast_to(place[j:j + 1, :], (8, LANES)) for j in range(tiles)], axis=1)

        def some(i, acc):
            start = pl.multiple_of(i * chunk * 8, chunk * 8)
            d = jnp.dot(cat_ref[pl.ds(start, chunk * 8), :], onehot, preferred_element_type=F32)
            for b in range(chunk):
                kb = jnp.broadcast_to(key_ref[pl.ds(i * chunk + b, 1), :], (8, LANES))
                kb = jnp.concatenate([kb] * tiles, axis=1)
                acc = acc + jnp.where(want == kb, d[b * 8:(b + 1) * 8], 0.0)
            return acc

        return lax.fori_loop(0, nblk // chunk, some, jnp.zeros((8, cols), F32))

    def give(k, carry):
        gbuf[k] = pick(k)
        copy_g(k).start()
        return carry

    lax.fori_loop(1, nsurf, give, 0)
    own = pick(0)

    def take(k, total):
        copy_g(k).wait()
        return total + rbuf[k]

    src_ref[...] = lax.fori_loop(1, nsurf, take, own)
    for p in range(PIECES):
        copy_a(p).wait_send()
        copy_s(p).wait_send()
        for k in range(1, chips):
            copy_b(k, p).wait_send()


def wall_source(profile, wall_weight, block_dest, col_face, bound_weight):
    nsurf = lax.axis_size("surf")
    chips = lax.axis_size("normal") // 2
    rows, nvars, faces = profile.shape
    outc = wall_weight.shape[0]
    comp = bound_weight.shape[0]
    w = wall_weight.reshape(outc, rows * nvars)
    extra = outc - 8
    w = jnp.concatenate([w[:8]] + [w[8:]] * (8 // extra), axis=0)
    nblk = faces // LANES
    cols = col_face.shape[0]
    length = faces // 2 // PIECES
    packed = length + length // (8 // extra)
    vmem = lambda: pl.BlockSpec(memory_space=pltpu.VMEM)
    dma = pltpu.SemaphoreType.DMA
    piece = (PIECES, 8, packed)
    return pl.pallas_call(
        functools.partial(source_kernel, nsurf, chips, outc),
        out_shape=jax.ShapeDtypeStruct((comp, cols), F32),
        in_specs=[vmem() for _ in range(5)],
        out_specs=vmem(),
        scratch_shapes=[
            pltpu.VMEM(piece, F32), pltpu.VMEM(piece, F32), pltpu.VMEM(piece, F32), pltpu.VMEM(piece, F32),
            pltpu.VMEM((chips - 1,) + piece, F32), pltpu.VMEM(piece, F32),
            pltpu.VMEM((nblk * 8, LANES), F32), pltpu.VMEM((nblk * 8, 2 * LANES), BF),
            pltpu.VMEM((nblk, LANES), jnp.int32), pltpu.VMEM((nsurf, cols // LANES, LANES), jnp.int32),
            pltpu.VMEM((nsurf, comp, cols), F32), pltpu.VMEM((nsurf, comp, cols), F32),
            dma((PIECES,)), dma((PIECES,)), dma((chips - 1, PIECES)), dma((chips - 1, PIECES)),
            dma((PIECES,)), dma((PIECES,)), dma((nsurf,)), dma((nsurf,)), dma((nsurf,)), dma((nsurf,)),
        ],
        compiler_params=pltpu.CompilerParams(
            collective_id=0, has_side_effects=True, vmem_limit_bytes=56 * 2**20),
        name="wall_source",
    )(profile, w, block_dest.reshape(nsurf, nblk), col_face.reshape(cols // LANES, LANES), bound_weight)


def char_kernel(sub, react_ref, inv_ref, src_ref, st_ref, out_ref, mix_ref, pair_ref, t_ref, dr_ref):
    comp, depth, width = st_ref.shape
    grp = 256 // comp

    @pl.when(pl.program_id(0) == 0)
    def _():
        half = 0.5 * react_ref[...]
        hi = half.astype(BF)
        lo = (half - hi.astype(F32)).astype(BF)
        down = lax.broadcasted_iota(jnp.int32, (256, comp), 0) // grp == lax.broadcasted_iota(jnp.int32, (256, comp), 1)
        over = lax.broadcasted_iota(jnp.int32, (comp, 256), 1) // grp == lax.broadcasted_iota(jnp.int32, (comp, 256), 0)
        down = jnp.where(down, 1.0, 0.0).astype(BF)
        over = jnp.where(over, 1.0, 0.0).astype(BF)
        r = lax.broadcasted_iota(jnp.int32, (256, 256), 0)
        c = lax.broadcasted_iota(jnp.int32, (256, 256), 1)
        same = r % grp == c % grp
        for i, part in enumerate((hi, lo)):
            rows = jnp.dot(down, part, preferred_element_type=F32).astype(BF)
            full = jnp.dot(rows, over, preferred_element_type=F32)
            mix_ref[:, i * 256:(i + 1) * 256] = jnp.where(same, full, 0.0).astype(BF)
        pair_ref[...] = jnp.zeros_like(pair_ref)
        pair_ref[:depth, :depth] = inv_ref[...]
        pair_ref[depth:, depth:] = inv_ref[...]

    lead = inv_ref[:, 0:1].astype(F32)
    for c in range(comp):
        t_ref[c] = jnp.tanh(st_ref[c]).astype(BF)
        out_ref[c] = st_ref[c]

    def step(i, carry):
        for h in range(width // sub):
            ls = slice(h * sub, (h + 1) * sub)
            for g in range(depth // grp):
                ds = slice(g * grp, (g + 1) * grp)
                t = t_ref[:, ds, ls].reshape(comp * grp, sub)
                m = jnp.dot(mix_ref[...], jnp.concatenate([t, t], axis=0), preferred_element_type=F32)
                dr_ref[:, ds, ls] = (out_ref[:, ds, ls] + m.reshape(comp, grp, sub)).astype(BF)
        for h in range(width // sub):
            ls = slice(h * sub, (h + 1) * sub)
            for p in range(comp // 2):
                x = dr_ref[2 * p:2 * p + 2, :, ls].reshape(2 * depth, sub)
                n2 = jnp.dot(pair_ref[...], x, preferred_element_type=F32)
                for k in range(2):
                    c = 2 * p + k
                    n = n2[k * depth:(k + 1) * depth] + lead * src_ref[c:c + 1, ls]
                    out_ref[c, :, ls] = n
                    t_ref[c, :, ls] = jnp.tanh(n).astype(BF)
        return carry

    lax.fori_loop(0, STEPS, step, 0)


def char_steps(char_state, source, char_inverse, react, tile=512, sub=256):
    comp, depth, cols = char_state.shape
    full = lambda a: pl.BlockSpec(a.shape, lambda i: (0,) * a.ndim)
    block = pl.BlockSpec((comp, depth, tile), lambda i: (0, 0, i))
    return pl.pallas_call(
        functools.partial(char_kernel, sub),
        grid=(cols // tile,),
        in_specs=[full(react), full(char_inverse), pl.BlockSpec((comp, tile), lambda i: (0, i)), block],
        out_specs=block,
        out_shape=jax.ShapeDtypeStruct(char_state.shape, F32),
        scratch_shapes=[
            pltpu.VMEM((256, 512), BF), pltpu.VMEM((2 * depth, 2 * depth), BF),
            pltpu.VMEM((comp, depth, tile), BF), pltpu.VMEM((comp, depth, tile), BF),
        ],
        compiler_params=pltpu.CompilerParams(vmem_limit_bytes=56 * 2**20),
        name="char_steps",
    )(react, char_inverse, source, char_state)


def body(profile, wall_weight, block_dest, col_face, char_state, char_inverse, react, bound_weight):
    source = wall_source(profile, wall_weight, block_dest, col_face, bound_weight)
    return char_steps(char_state, source, char_inverse, react)


def solution(mesh):
    placed = (
        P("normal", None, "surf"),
        P(None, "normal", None),
        P(),
        P(("surf", "normal")),
        P(None, None, ("surf", "normal")),
        P(),
        P(),
        P(),
    )
    return jax.shard_map(
        body,
        mesh=mesh,
        in_specs=placed,
        out_specs=P(None, None, ("surf", "normal")),
        check_vma=False,
    )
```

```python
import functools

import jax
import jax.numpy as jnp
from jax import lax
from jax.experimental import pallas as pl
from jax.experimental.pallas import tpu as pltpu
from jax.sharding import PartitionSpec as P

STEPS = 8
PIECES = 4
LANES = 128
F32 = jnp.float32
BF = jnp.bfloat16
MESH = pl.DeviceIdType.MESH


def source_kernel(
    nsurf, chips, outc,
    x_ref, w_ref, dest_ref, cf_ref, bw_ref,
    src_ref,
    send_a, own_a, recv_a, chip_b, recv_b, wall_ref, s_ref, cat_ref, key_ref, cf_all, gbuf, rbuf,
    sa_send, sa_recv, sb_send, sb_recv, ss_send, ss_recv, sc_send, sc_recv, sg_send, sg_recv,
):
    surf = lax.axis_index("surf")
    normal = lax.axis_index("normal")
    y, core = normal // 2, normal % 2
    peer = (surf, y * 2 + 1 - core)
    extra = outc - 8
    subs = 8 // extra
    faces = x_ref.shape[2]
    half = faces // 2
    piece = half // PIECES
    sub = piece // subs
    depth = x_ref.shape[0] * x_ref.shape[1]
    nblk = faces // LANES
    groups = piece // LANES

    def chip_peer(k):
        return (surf, lax.rem(y + k, chips) * 2 + core)

    def surf_peer(k):
        return (lax.rem(surf + k, nsurf), normal)

    barrier = pltpu.get_barrier_semaphore()
    pl.semaphore_signal(barrier, inc=1, device_id=peer, device_id_type=MESH)
    for k in range(1, chips):
        pl.semaphore_signal(barrier, inc=1, device_id=chip_peer(k), device_id_type=MESH)

    def greet(k, carry):
        pl.semaphore_signal(barrier, inc=1, device_id=surf_peer(k), device_id_type=MESH)
        return carry

    lax.fori_loop(1, nsurf, greet, 0)

    wide = w_ref[...].astype(F32)
    row = lax.broadcasted_iota(jnp.int32, (8, depth), 0)

    def weights(q):
        below = jnp.zeros((8, depth), F32)
        for e in range(extra):
            line = jnp.broadcast_to(wide[8 + e:9 + e], (8, depth))
            below = jnp.where(row == q * extra + e, line, below)
        return jnp.concatenate([wide[:8], below], axis=0).astype(BF)

    placed = [weights(q) for q in range(subs)]

    def partial(which, p):
        rest = None
        main = []
        for q in range(subs):
            start = pl.multiple_of(which * half + p * piece + q * sub, sub)
            x = x_ref[:, :, pl.ds(start, sub)].reshape(depth, sub)
            r = jnp.dot(placed[q], x, preferred_element_type=F32)
            main.append(r[:8])
            rest = r[8:] if rest is None else rest + r[8:]
        return jnp.concatenate(main + [rest], axis=1)

    def copy_a(p):
        return pltpu.make_async_remote_copy(
            src_ref=send_a.at[p], dst_ref=recv_a.at[p], send_sem=sa_send.at[p], recv_sem=sa_recv.at[p],
            device_id=peer, device_id_type=MESH)

    def copy_b(k, p):
        return pltpu.make_async_remote_copy(
            src_ref=chip_b.at[p], dst_ref=recv_b.at[k - 1, p], send_sem=sb_send.at[k - 1, p],
            recv_sem=sb_recv.at[k - 1, p], device_id=chip_peer(k), device_id_type=MESH)

    def copy_s(p):
        start = pl.multiple_of((core * PIECES + p) * groups * 8, groups * 8)
        rows = s_ref.at[pl.ds(start, groups * 8)]
        return pltpu.make_async_remote_copy(
            src_ref=rows, dst_ref=rows, send_sem=ss_send.at[p], recv_sem=ss_recv.at[p],
            device_id=peer, device_id_type=MESH)

    def wait_s(p):
        start = pl.multiple_of(((1 - core) * PIECES + p) * groups * 8, groups * 8)
        rows = s_ref.at[pl.ds(start, groups * 8)]
        return pltpu.make_async_remote_copy(
            src_ref=rows, dst_ref=rows, send_sem=ss_send.at[p], recv_sem=ss_recv.at[p],
            device_id=peer, device_id_type=MESH)

    def copy_c(k):
        return pltpu.make_async_remote_copy(
            src_ref=cf_ref, dst_ref=cf_all.at[k], send_sem=sc_send.at[k], recv_sem=sc_recv.at[k],
            device_id=surf_peer(k), device_id_type=MESH)

    def copy_g(k):
        return pltpu.make_async_remote_copy(
            src_ref=gbuf.at[k], dst_ref=rbuf.at[k], send_sem=sg_send.at[k], recv_sem=sg_recv.at[k],
            device_id=surf_peer(k), device_id_type=MESH)

    send_a[0] = partial(1 - core, 0)
    pl.semaphore_wait(barrier, 1 + chips - 1 + nsurf - 1)
    copy_a(0).start()
    own_a[0] = partial(core, 0)
    for p in range(1, PIECES):
        send_a[p] = partial(1 - core, p)
        copy_a(p).start()
        own_a[p] = partial(core, p)
    for p in range(PIECES):
        copy_a(p).wait_recv()
        chip_b[p] = own_a[p] + recv_a[p]
        for k in range(1, chips):
            copy_b(k, p).start()

    def start_c(k, carry):
        copy_c(k).start()
        return carry

    lax.fori_loop(1, nsurf, start_c, 0)
    cf_all[0] = cf_ref[...]

    line = lax.broadcasted_iota(jnp.int32, (nblk, nblk), 0)
    lane = lax.broadcasted_iota(jnp.int32, (nblk, nblk), 1)
    mine = jnp.broadcast_to(dest_ref[pl.ds(surf, 1), :], (nblk, nblk))
    owner = jnp.sum(jnp.where(line == lane, mine, 0), axis=1, keepdims=True)

    def count(s, total):
        other = jnp.broadcast_to(dest_ref[pl.ds(s, 1), :], (nblk, nblk))
        before = s * nblk + lane < surf * nblk + line
        return total + jnp.where(jnp.logical_and(other == owner, before), 1, 0)

    ranks = lax.fori_loop(0, nsurf, count, jnp.zeros((nblk, nblk), jnp.int32))
    rank = jnp.sum(ranks, axis=1, keepdims=True)
    key_ref[...] = jnp.broadcast_to(owner * nblk + rank, (nblk, LANES))

    bw = bw_ref[...]
    columns = [jnp.broadcast_to(bw[:, o:o + 1], (8, sub)) for o in range(outc)]
    for p in range(PIECES):
        total = chip_b[p]
        for k in range(1, chips):
            copy_b(k, p).wait_recv()
            total = total + recv_b[k - 1, p]
        wall_ref[p] = total * lax.rsqrt(1.0 + total * total)
        for q in range(subs):
            acc = jnp.zeros((8, sub), F32)
            for o in range(outc):
                if o < 8:
                    w = wall_ref[p, o:o + 1, q * sub:(q + 1) * sub]
                else:
                    r = q * extra + o - 8
                    w = wall_ref[p, r:r + 1, piece:piece + sub]
                acc = acc + columns[o] * jnp.broadcast_to(w, (8, sub))
            for i in range(sub // LANES):
                at = (core * PIECES + p) * groups + q * (sub // LANES) + i
                s_ref[pl.ds(pl.multiple_of(at * 8, 8), 8), :] = acc[:, i * LANES:(i + 1) * LANES]
        copy_s(p).start()

    def split(start, rows):
        s = s_ref[pl.ds(start, rows), :]
        hi = s.astype(BF)
        cat_ref[pl.ds(start, rows), :] = jnp.concatenate(
            [hi, (s - hi.astype(F32)).astype(BF)], axis=1)

    for p in range(PIECES):
        split(pl.multiple_of((core * PIECES + p) * groups * 8, groups * 8), groups * 8)

    def wait_c(k, carry):
        copy_c(k).wait()
        return carry

    lax.fori_loop(1, nsurf, wait_c, 0)
    for p in range(PIECES):
        wait_s(p).wait_recv()
        split(pl.multiple_of(((1 - core) * PIECES + p) * groups * 8, groups * 8), groups * 8)

    tiles = cf_ref.shape[0]
    cols = tiles * LANES
    within = lax.broadcasted_iota(jnp.int32, (LANES, LANES), 0)
    chunk = 32

    def pick(k):
        who = lax.rem(surf + k, nsurf)
        cf = cf_all[lax.rem(nsurf - k, nsurf)]
        place = who * nblk + cf // LANES
        spot = cf % LANES
        onehot = jnp.concatenate(
            [jnp.where(within == spot[j:j + 1, :], 1.0, 0.0).astype(BF) for j in range(tiles)], axis=1)
        onehot = jnp.concatenate([onehot, onehot], axis=0)
        want = jnp.concatenate(
            [jnp.broadcast_to(place[j:j + 1, :], (8, LANES)) for j in range(tiles)], axis=1)

        def some(i, acc):
            start = pl.multiple_of(i * chunk * 8, chunk * 8)
            d = jnp.dot(cat_ref[pl.ds(start, chunk * 8), :], onehot, preferred_element_type=F32)
            for b in range(chunk):
                kb = jnp.broadcast_to(key_ref[pl.ds(i * chunk + b, 1), :], (8, LANES))
                kb = jnp.concatenate([kb] * tiles, axis=1)
                acc = acc + jnp.where(want == kb, d[b * 8:(b + 1) * 8], 0.0)
            return acc

        return lax.fori_loop(0, nblk // chunk, some, jnp.zeros((8, cols), F32))

    def give(i, carry):
        k = nsurf // 2 + (1 - 2 * lax.rem(i + 1, 2)) * (i // 2)
        gbuf[k] = pick(k)
        copy_g(k).start()
        return carry

    lax.fori_loop(1, nsurf, give, 0)
    own = pick(0)

    def take(k, total):
        copy_g(k).wait()
        return total + rbuf[k]

    src_ref[...] = lax.fori_loop(1, nsurf, take, own)
    for p in range(PIECES):
        copy_a(p).wait_send()
        copy_s(p).wait_send()
        for k in range(1, chips):
            copy_b(k, p).wait_send()


def wall_source(profile, wall_weight, block_dest, col_face, bound_weight):
    nsurf = lax.axis_size("surf")
    chips = lax.axis_size("normal") // 2
    rows, nvars, faces = profile.shape
    outc = wall_weight.shape[0]
    comp = bound_weight.shape[0]
    w = wall_weight.reshape(outc, rows * nvars)
    extra = outc - 8
    nblk = faces // LANES
    cols = col_face.shape[0]
    length = faces // 2 // PIECES
    packed = length + length // (8 // extra)
    vmem = lambda: pl.BlockSpec(memory_space=pltpu.VMEM)
    dma = pltpu.SemaphoreType.DMA
    piece = (PIECES, 8, packed)
    return pl.pallas_call(
        functools.partial(source_kernel, nsurf, chips, outc),
        out_shape=jax.ShapeDtypeStruct((comp, cols), F32),
        in_specs=[vmem() for _ in range(5)],
        out_specs=vmem(),
        scratch_shapes=[
            pltpu.VMEM(piece, F32), pltpu.VMEM(piece, F32), pltpu.VMEM(piece, F32), pltpu.VMEM(piece, F32),
            pltpu.VMEM((chips - 1,) + piece, F32), pltpu.VMEM(piece, F32),
            pltpu.VMEM((nblk * 8, LANES), F32), pltpu.VMEM((nblk * 8, 2 * LANES), BF),
            pltpu.VMEM((nblk, LANES), jnp.int32), pltpu.VMEM((nsurf, cols // LANES, LANES), jnp.int32),
            pltpu.VMEM((nsurf, comp, cols), F32), pltpu.VMEM((nsurf, comp, cols), F32),
            dma((PIECES,)), dma((PIECES,)), dma((chips - 1, PIECES)), dma((chips - 1, PIECES)),
            dma((PIECES,)), dma((PIECES,)), dma((nsurf,)), dma((nsurf,)), dma((nsurf,)), dma((nsurf,)),
        ],
        compiler_params=pltpu.CompilerParams(
            collective_id=0, has_side_effects=True, vmem_limit_bytes=56 * 2**20),
        name="wall_source",
    )(profile, w, block_dest.reshape(nsurf, nblk), col_face.reshape(cols // LANES, LANES), bound_weight)


def char_kernel(sub, react_ref, inv_ref, src_ref, st_ref, out_ref, mix_ref, pair_ref, t_ref, dr_ref):
    comp, depth, width = st_ref.shape
    grp = 128 // comp
    size = grp * comp

    @pl.when(pl.program_id(0) == 0)
    def _():
        half = 0.5 * react_ref[...]
        hi = half.astype(BF)
        lo = (half - hi.astype(F32)).astype(BF)
        down = lax.broadcasted_iota(jnp.int32, (size, comp), 0) // grp == lax.broadcasted_iota(jnp.int32, (size, comp), 1)
        over = lax.broadcasted_iota(jnp.int32, (comp, size), 1) // grp == lax.broadcasted_iota(jnp.int32, (comp, size), 0)
        down = jnp.where(down, 1.0, 0.0).astype(BF)
        over = jnp.where(over, 1.0, 0.0).astype(BF)
        r = lax.broadcasted_iota(jnp.int32, (size, size), 0)
        c = lax.broadcasted_iota(jnp.int32, (size, size), 1)
        same = r % grp == c % grp
        for i, part in enumerate((hi, lo)):
            rows = jnp.dot(down, part, preferred_element_type=F32).astype(BF)
            full = jnp.dot(rows, over, preferred_element_type=F32)
            mix_ref[:, i * size:(i + 1) * size] = jnp.where(same, full, 0.0).astype(BF)
        pair_ref[...] = jnp.zeros_like(pair_ref)
        pair_ref[:depth, :depth] = inv_ref[...]
        pair_ref[depth:, depth:] = inv_ref[...]

    lead = inv_ref[:, 0:1].astype(F32)
    for c in range(comp):
        t_ref[c] = jnp.tanh(st_ref[c]).astype(BF)
        out_ref[c] = st_ref[c]

    def step(i, carry):
        for h in range(width // sub):
            ls = slice(h * sub, (h + 1) * sub)
            for g in range(depth // grp):
                ds = slice(g * grp, (g + 1) * grp)
                t = t_ref[:, ds, ls].reshape(comp * grp, sub)
                m = jnp.dot(mix_ref[...], jnp.concatenate([t, t], axis=0), preferred_element_type=F32)
                dr_ref[:, ds, ls] = (out_ref[:, ds, ls] + m.reshape(comp, grp, sub)).astype(BF)
        for h in range(width // sub):
            ls = slice(h * sub, (h + 1) * sub)
            for p in range(comp // 2):
                x = dr_ref[2 * p:2 * p + 2, :, ls].reshape(2 * depth, sub)
                n2 = jnp.dot(pair_ref[...], x, preferred_element_type=F32)
                for k in range(2):
                    c = 2 * p + k
                    n = n2[k * depth:(k + 1) * depth] + lead * src_ref[c:c + 1, ls]
                    out_ref[c, :, ls] = n
                    t_ref[c, :, ls] = jnp.tanh(n).astype(BF)
        return carry

    lax.fori_loop(0, STEPS, step, 0, unroll=STEPS)


def char_steps(char_state, source, char_inverse, react, tile=512, sub=256):
    comp, depth, cols = char_state.shape
    full = lambda a: pl.BlockSpec(a.shape, lambda i: (0,) * a.ndim)
    block = pl.BlockSpec((comp, depth, tile), lambda i: (0, 0, i))
    return pl.pallas_call(
        functools.partial(char_kernel, sub),
        grid=(cols // tile,),
        in_specs=[full(react), full(char_inverse), pl.BlockSpec((comp, tile), lambda i: (0, i)), block],
        out_specs=block,
        out_shape=jax.ShapeDtypeStruct(char_state.shape, F32),
        scratch_shapes=[
            pltpu.VMEM((128, 256), BF), pltpu.VMEM((2 * depth, 2 * depth), BF),
            pltpu.VMEM((comp, depth, tile), BF), pltpu.VMEM((comp, depth, tile), BF),
        ],
        compiler_params=pltpu.CompilerParams(vmem_limit_bytes=56 * 2**20),
        name="char_steps",
    )(react, char_inverse, source, char_state)


def body(profile, wall_weight, block_dest, col_face, char_state, char_inverse, react, bound_weight):
    source = wall_source(profile, wall_weight, block_dest, col_face, bound_weight)
    return char_steps(char_state, source, char_inverse, react)


def solution(mesh):
    placed = (
        P("normal", None, "surf"),
        P(None, "normal", None),
        P(),
        P(("surf", "normal")),
        P(None, None, ("surf", "normal")),
        P(),
        P(),
        P(),
    )
    return jax.shard_map(
        body,
        mesh=mesh,
        in_specs=placed,
        out_specs=P(None, None, ("surf", "normal")),
        check_vma=False,
    )
```
